32 devices in a mesh: parts: 2 (over x), wide: 16 (over z, y, core).
Axes of the slice: x: 2, y: 2, z: 4, core: 2. Of those that a mesh axis runs over, the one named last changes fastest.
Arguments:
- embeddings: bfloat16 [16384, 768], P(('parts', 'wide')), parts along dimension 0, may hold values from -48 to 48
- cluster_of: int32 [16384], P(('parts', 'wide')), parts along dimension 0, may hold values from 0 to 7, as said below
- sharpness: float32 [16], P('parts'), parts along dimension 0, may hold values from 2 to 16
Outputs:
- density: float32 [16384], P(('parts', 'wide')), parts along dimension 0
The draws below stay inside these ranges and needn't reach their ends.
There are 2 independent parts, one for each index of `parts`. The reference program is written for one: setup_inputs(seed, part) draws one part's arguments, and reference() takes and returns one part's arrays. A program takes and returns all parts, laid end to end along the dimension named above; each array names one. Nothing has to cross between parts.
Inputs may be any that keep to these rules, and one draw needn't show every extreme that they name: `cluster_of`: in the rows of one device no cluster occurs more than 128 times; one and the same cluster occurs exactly 128 times in the rows of every device, and every cluster occurs in the rows of every device.
All inputs are finite; a program needn't handle non-finite values.
Results may differ from the reference program's by a relative error of at most 0.0003.
Values may be sent and summed in bfloat16 or wider, within the bound.
A program may use at most 64 MiB of HBM per device.

```python
import math
import jax
import jax.numpy as jnp
from jax import lax

E = 768
ROWS_DEV = 512
CLUSTERS = 8
MOST = 128
N_WIDE = 16


def cluster_draw(key):
    key = jax.random.fold_in(key, 101)
    sub_keys = jax.random.split(key, 4)
    slot_total = CLUSTERS * MOST
    lean_levels = jax.random.randint(sub_keys[0], (CLUSTERS,), 0, 4)
    full_cluster = jax.random.randint(sub_keys[1], (), 0, CLUSTERS)
    slot_ids = jnp.arange(slot_total, dtype=jnp.int32)
    slot_owner = slot_ids // MOST
    jitter_draw = jax.random.randint(sub_keys[2], (N_WIDE, slot_total), 0, 2 ** 14)
    slot_score = jitter_draw + lean_levels[slot_owner][None, :] * 2 ** 12
    forced = (slot_ids % MOST == 0) | (slot_owner == full_cluster)
    slot_score = jnp.where(forced[None, :], 2 ** 15, slot_score)
    slot_score = slot_score * slot_total + slot_ids[None, :]
    ranked = jnp.argsort(-slot_score, axis=1, stable=True)[:, :ROWS_DEV]
    chosen = (ranked // MOST).astype(jnp.int32)

    def shuffle_order(sub_key):
        return jax.random.permutation(sub_key, ROWS_DEV)
    orders = jax.vmap(shuffle_order)(jax.random.split(sub_keys[3], N_WIDE))
    shuffled = jnp.take_along_axis(chosen, orders, axis=1)
    return shuffled.reshape(N_WIDE * ROWS_DEV).astype(jnp.int32)


def draw_cluster_of(key, part):
    return cluster_draw(key)


def draw_embeddings(key, part):
    membership = cluster_draw(key)
    key = jax.random.fold_in(key, 3)
    sub_keys = jax.random.split(key, 10)

    def component(base_key, row_ids):

        def one_row(index):
            return jnp.clip(jax.random.normal(jax.random.fold_in(base_key, index), (E,), jnp.float32), -5.0, 5.0)
        return jax.vmap(one_row)(row_ids)
    top_scale = 10.0
    row_total = ROWS_DEV * N_WIDE
    families = max(ROWS_DEV // 4, 1)
    doc_ids = jnp.arange(row_total, dtype=jnp.int32)
    sub_choice = jax.random.randint(sub_keys[0], (row_total,), 0, 32)
    near_flag = jax.random.randint(sub_keys[1], (row_total,), 0, 10) < 4
    family_choice = jax.random.randint(sub_keys[2], (row_total,), 0, families)
    family_ids = jnp.where(near_flag, membership * families + family_choice, CLUSTERS * families + doc_ids).astype(jnp.int32)
    centre_weight = jax.random.uniform(sub_keys[3], (CLUSTERS,), jnp.float32, 0.45, 0.7)[membership]
    family_weight = jnp.sqrt(0.75 - centre_weight * centre_weight)
    noise_weight = jnp.exp(jax.random.uniform(sub_keys[4], (row_total, 1), jnp.float32, math.log(0.12), math.log(0.5)))
    row_scales = jnp.exp(jax.random.uniform(sub_keys[5], (row_total, 1), jnp.float32, 0.0, math.log(top_scale)))
    values = centre_weight[:, None] * component(sub_keys[6], membership)
    values = values + 0.5 * component(sub_keys[7], membership * 32 + sub_choice)
    values = values + family_weight[:, None] * component(sub_keys[8], family_ids)
    values = values + noise_weight * component(sub_keys[9], doc_ids)
    values = jnp.clip(row_scales * values, -48.0, 48.0)
    return values.astype(jnp.bfloat16)


def setup_inputs(seed: int = 0, part: int = 0) -> dict:
    key_list = jax.random.split(jax.random.key(seed), 4)
    part_keys = jax.random.split(jax.random.fold_in(key_list[3], part), 4)
    return {
        "embeddings": draw_embeddings(jax.random.fold_in(jax.random.fold_in(key_list[3], part), 71), part),
        "cluster_of": draw_cluster_of(jax.random.fold_in(jax.random.fold_in(key_list[3], part), 71), part),
        "sharpness": jnp.clip(jnp.exp(jax.random.uniform(part_keys[2], (CLUSTERS,), jnp.float32, math.log(2.0), math.log(16.0))), 2.0, 16.0),
    }


EPSILON = 1e-06

def unit_rows(embeddings):
    values = embeddings.astype(jnp.float32)
    scaled = values * lax.rsqrt(lax.optimization_barrier(jnp.sum(values * values, axis=1, keepdims=True)) + EPSILON)
    return scaled.astype(jnp.bfloat16)

def reference(embeddings, cluster_of, sharpness):
    unit_vectors = unit_rows(embeddings)
    total = embeddings.shape[0]
    sorted_index = jnp.argsort(cluster_of, stable=True).astype(jnp.int32)
    sorted_units = unit_vectors[sorted_index]
    sorted_ids = cluster_of[sorted_index].astype(jnp.int32)
    member_count = jax.ops.segment_sum(jnp.ones_like(cluster_of), cluster_of, num_segments=CLUSTERS).astype(jnp.int32)
    starts = (jnp.cumsum(member_count) - member_count).astype(jnp.int32)
    reach = 512 + 2 * N_WIDE * MOST
    padded_units = jnp.concatenate([sorted_units, jnp.zeros((reach, E), jnp.bfloat16)], axis=0)
    padded_ids = jnp.concatenate([sorted_ids, jnp.full((reach,), -1, jnp.int32)], axis=0)
    row_offsets = jnp.arange(512, dtype=jnp.int32)
    column_offsets = jnp.arange(reach, dtype=jnp.int32)

    def one_block(block_index):
        first = (block_index * 512).astype(jnp.int32)
        rows_here = lax.dynamic_slice_in_dim(sorted_units, first, 512, 0)
        ids_here = lax.dynamic_slice_in_dim(sorted_ids, first, 512, 0)
        window_start = starts[ids_here[0]].astype(jnp.int32)
        window = lax.dynamic_slice_in_dim(padded_units, window_start, reach, 0)
        window_ids = lax.dynamic_slice_in_dim(padded_ids, window_start, reach, 0)
        similarity = jnp.dot(rows_here, window.T, preferred_element_type=jnp.float32)
        kernel = jnp.exp(sharpness[ids_here][:, None] * (similarity - 1.0))
        same = (ids_here[:, None] == window_ids[None, :]) & ((first + row_offsets)[:, None] != (window_start + column_offsets)[None, :])
        kernel_total = lax.optimization_barrier(jnp.sum(jnp.where(same, kernel, 0.0), axis=1))
        divisor = jnp.maximum(member_count[ids_here] - 1, 1).astype(jnp.float32)
        return jnp.log(kernel_total / divisor)
    sorted_density = lax.map(one_block, jnp.arange(total // 512, dtype=jnp.int32)).reshape(total)
    return jnp.zeros((total,), jnp.float32).at[sorted_index].set(sorted_density)
```

```python
import functools

import jax
import jax.numpy as jnp
from jax import lax
from jax.experimental import pallas as pl
from jax.experimental.pallas import tpu as pltpu
from jax.sharding import PartitionSpec as P

EPSILON = 1e-06
LOG2E = 1.4426950408889634
DEAD = -1e30
LANES = 128
GROUP_ROWS = 256
MESH = pl.DeviceIdType.MESH


def flipped(value, mask, bits):
    out = 0
    for k in range(bits):
        left = (value // (1 << k)) % 2
        right = (mask // (1 << k)) % 2
        out = out + (left + right - 2 * left * right) * (1 << k)
    return out


def body(
    devices, clusters, cap,
    emb_ref, cluster_ref, sharp_ref, out_ref,
    unit, send, own, other, count_out, count_in, own_bias, other_bias, total, back_out, back_in,
    row_send, row_recv, count_send, count_recv, pass_send, pass_recv, back_send, back_recv,
):
    bits = devices.bit_length() - 1
    me = lax.axis_index("wide")
    rows, width = emb_ref.shape
    fan = GROUP_ROWS // cap
    groups = devices // fan
    group_bits = groups.bit_length() - 1
    my_group = me // fan
    half = me % 2
    partner = me + 1 - 2 * half
    my_cluster = me // 2

    def peer(mask):
        return flipped(me, mask, bits)

    def group_of(mask):
        return flipped(my_group, mask, group_bits)

    barrier = pltpu.get_barrier_semaphore()
    for mask in range(1, devices):
        pl.semaphore_signal(barrier, inc=1, device_id={"wide": peer(mask)}, device_id_type=MESH)

    cluster = cluster_ref[...]
    onehot = lax.broadcasted_iota(jnp.int32, (clusters, rows), 0) == cluster
    ones = jnp.where(onehot, 1.0, 0.0)
    before = (
        lax.broadcasted_iota(jnp.int32, (rows, rows), 0)
        < lax.broadcasted_iota(jnp.int32, (rows, rows), 1)
    )
    prefix = jnp.dot(
        ones.astype(jnp.bfloat16),
        jnp.where(before, 1.0, 0.0).astype(jnp.bfloat16),
        preferred_element_type=jnp.float32,
    )
    within = jnp.sum(prefix * ones, axis=0, keepdims=True).astype(jnp.int32)
    target = 2 * cluster + (within & 1)
    place = within >> 1
    position = target * cap + place
    counts = jnp.broadcast_to(jnp.sum(ones, axis=1, keepdims=True), (clusters, LANES))
    for c in range(clusters):
        count_out[c] = jnp.broadcast_to(counts[c : c + 1], (8, LANES))

    values = emb_ref[...].astype(jnp.float32)
    scale = lax.rsqrt(jnp.sum(values * values, axis=1, keepdims=True) + EPSILON)
    unit[...] = (values * scale).astype(jnp.bfloat16)

    pl.semaphore_wait(barrier, devices - 1)

    def count_copy(mask):
        to = peer(mask)
        return pltpu.make_async_remote_copy(
            src_ref=count_out.at[to // 2], dst_ref=count_in.at[me],
            send_sem=count_send.at[mask], recv_sem=count_recv.at[mask],
            device_id={"wide": to}, device_id_type=MESH,
        )

    def row_copy(mask):
        to = peer(mask)
        return pltpu.make_async_remote_copy(
            src_ref=send.at[to], dst_ref=own.at[me],
            send_sem=row_send.at[mask], recv_sem=row_recv.at[mask],
            device_id={"wide": to}, device_id_type=MESH,
        )

    def pass_copy(mask, landing):
        origin = peer(mask)
        return pltpu.make_async_remote_copy(
            src_ref=own.at[origin], dst_ref=other.at[origin],
            send_sem=pass_send.at[mask], recv_sem=pass_recv.at[landing],
            device_id={"wide": partner}, device_id_type=MESH,
        )

    def back_copy(mask):
        to = peer(mask)
        return pltpu.make_async_remote_copy(
            src_ref=back_out.at[(to * cap) // LANES], dst_ref=back_in.at[me],
            send_sem=back_send.at[mask], recv_sem=back_recv.at[mask],
            device_id={"wide": to}, device_id_type=MESH,
        )

    for step in reversed(range(groups)):
        goal = group_of(step)
        slot = lax.broadcasted_iota(jnp.int32, (GROUP_ROWS, rows), 0) + goal * GROUP_ROWS
        pick = jnp.where(slot == position, 1.0, 0.0).astype(jnp.bfloat16)
        packed = jnp.dot(pick, unit[...], preferred_element_type=jnp.float32)
        send[pl.ds(goal * fan, fan)] = packed.astype(jnp.bfloat16).reshape(fan, cap, width)
        for g in range(fan):
            mask = step * fan + g
            if mask:
                row_copy(mask).start()
            else:
                own[me] = send[me]
        if step == groups - 1:
            for mask in range(1, devices):
                count_copy(mask).start()
    count_in[me] = count_out[my_cluster]

    sharp = sharp_ref[my_cluster] * LOG2E
    total[...] = jnp.zeros_like(total)
    inner = lax.broadcasted_iota(jnp.int32, (cap, LANES), 0).astype(jnp.float32)
    skip = (
        lax.broadcasted_iota(jnp.int32, (GROUP_ROWS, GROUP_ROWS), 0)
        == lax.broadcasted_iota(jnp.int32, (GROUP_ROWS, GROUP_ROWS), 1)
    )
    half_f = half.astype(jnp.float32)

    def add_block(rows_ref, bias_ref, j, i, diagonal=False):
        left = rows_ref[pl.ds(j * fan, fan)].reshape(GROUP_ROWS, width)
        right = own[pl.ds(i * fan, fan)].reshape(GROUP_ROWS, width)
        similarity = lax.dot_general(
            left, right, (((1,), (1,)), ((), ())), preferred_element_type=jnp.float32
        )
        bias = bias_ref[pl.ds(j * fan, fan)].reshape(GROUP_ROWS, LANES)
        bias = jnp.concatenate([bias] * (GROUP_ROWS // LANES), axis=1)
        kernel = jnp.exp2(similarity * sharp + bias)
        if diagonal:
            kernel = jnp.where(skip, 0.0, kernel)
        total[i] += jnp.sum(kernel.reshape(GROUP_ROWS // 8, 8, GROUP_ROWS), axis=0)

    for step in range(groups):
        for g in range(fan):
            mask = step * fan + g
            if mask:
                row_copy(mask).wait_recv()
            pass_copy(mask, mask ^ 1).start()
        for g in range(fan):
            mask = step * fan + g
            origin = peer(mask)
            if mask:
                count_copy(mask).wait_recv()
            count = count_in[origin][0:1]
            own_live = jnp.floor((count + 1.0 - half_f) * 0.5)
            own_bias[origin] = jnp.where(inner < own_live, -sharp, DEAD)
            other_bias[origin] = jnp.where(inner < count - own_live, -sharp, DEAD)
        here = group_of(step)
        add_block(own, own_bias, here, here, diagonal=True)
        for g in range(fan):
            pass_copy(step * fan + g, step * fan + g).wait_recv()
        add_block(other, other_bias, here, here)
        if step:

            def earlier(index, carry):
                there = group_of(index)
                add_block(own, own_bias, here, there)
                add_block(other, other_bias, here, there)
                add_block(own, own_bias, there, here)
                add_block(other, other_bias, there, here)
                return carry

            lax.fori_loop(0, step, earlier, 0)

    members = jnp.sum(count_in[...], axis=0)[0:1]
    divisor = jnp.maximum(members - 1.0, 1.0)
    pieces = GROUP_ROWS // LANES
    for i in range(groups):
        sums = jnp.sum(total[i], axis=0, keepdims=True)
        for piece in range(pieces):
            density = jnp.log(sums[:, piece * LANES : (piece + 1) * LANES] / divisor)
            back_out[i * pieces + piece] = jnp.broadcast_to(density, (8, LANES))
    for mask in range(1, devices):
        back_copy(mask).start()
    back_in[me] = back_out[(me * cap) // LANES]

    lane = place + (me * cap) % LANES
    choose = jnp.where(lax.broadcasted_iota(jnp.int32, (LANES, rows), 0) == lane, 1.0, 0.0)
    mine = lax.broadcasted_iota(jnp.int32, (devices, rows), 0) == target
    for mask in range(1, devices):
        back_copy(mask).wait_recv()
    gathered = jnp.dot(
        back_in[...][:, 0, :], choose,
        preferred_element_type=jnp.float32, precision=lax.Precision.HIGHEST,
    )
    out_ref[...] = jnp.sum(jnp.where(mine, gathered, 0.0), axis=0, keepdims=True)

    for mask in range(devices):
        pass_copy(mask, mask ^ 1).wait_send()
        if mask:
            count_copy(mask).wait_send()
            row_copy(mask).wait_send()
            back_copy(mask).wait_send()


def per_device(embeddings, cluster_of, sharpness):
    devices = lax.axis_size("wide")
    rows, width = embeddings.shape
    clusters = sharpness.shape[0]
    cap = max(16, rows // clusters)
    slots = devices * cap
    vmem = pl.BlockSpec(memory_space=pltpu.VMEM)
    dma = pltpu.SemaphoreType.DMA((devices,))
    out = pl.pallas_call(
        functools.partial(body, devices, clusters, cap),
        out_shape=jax.ShapeDtypeStruct((1, rows), jnp.float32),
        in_specs=[vmem, vmem, pl.BlockSpec(memory_space=pltpu.SMEM)],
        out_specs=vmem,
        scratch_shapes=[
            pltpu.VMEM((rows, width), jnp.bfloat16),
            pltpu.VMEM((devices, cap, width), jnp.bfloat16),
            pltpu.VMEM((devices, cap, width), jnp.bfloat16),
            pltpu.VMEM((devices, cap, width), jnp.bfloat16),
            pltpu.VMEM((clusters, 8, LANES), jnp.float32),
            pltpu.VMEM((devices, 8, LANES), jnp.float32),
            pltpu.VMEM((devices, cap, LANES), jnp.float32),
            pltpu.VMEM((devices, cap, LANES), jnp.float32),
            pltpu.VMEM((slots // GROUP_ROWS, 8, GROUP_ROWS), jnp.float32),
            pltpu.VMEM((slots // LANES, 8, LANES), jnp.float32),
            pltpu.VMEM((devices, 8, LANES), jnp.float32),
            dma, dma, dma, dma, dma, dma, dma, dma,
        ],
        compiler_params=pltpu.CompilerParams(
            collective_id=0, has_side_effects=True, vmem_limit_bytes=40 * 1024 * 1024
        ),
    )(embeddings, cluster_of.reshape(1, rows), sharpness)
    return out.reshape(rows)


def solution(mesh):
    in_specs = (P(("parts", "wide"), None), P(("parts", "wide")), P("parts"))
    out_specs = P(("parts", "wide"))
    return jax.shard_map(
        per_device, mesh=mesh, in_specs=in_specs, out_specs=out_specs, check_vma=False
    )
```

```python
import functools

import jax
import jax.numpy as jnp
from jax import lax
from jax.experimental import pallas as pl
from jax.experimental.pallas import tpu as pltpu
from jax.sharding import PartitionSpec as P

EPSILON = 1e-06
LOG2E = 1.4426950408889634
DEAD = -1e30
LANES = 128
GROUP_ROWS = 256
MESH = pl.DeviceIdType.MESH
RANK_CAPS = (64, 64, 64, 64, 48, 48, 32, 32)
RANK_PLACES = (0, 4, 5, 1, 2, 6, 3, 7)


def flipped(value, mask, bits):
    out = 0
    for k in range(bits):
        left = (value // (1 << k)) % 2
        right = (mask // (1 << k)) % 2
        out = out + (left + right - 2 * left * right) * (1 << k)
    return out


def body(
    devices, clusters, cap, caps, places,
    emb_ref, cluster_ref, sharp_ref, out_ref, flag_ref,
    unit, send, own, other, count_out, count_in, home_count, own_bias, other_bias, total,
    back_out, back_in, flag_out, flag_in,
    row_send, row_recv, count_send, count_recv, pass_send, pass_recv, back_send, back_recv,
    flag_send, flag_recv,
):
    bits = devices.bit_length() - 1
    me = lax.axis_index("wide")
    rows, width = emb_ref.shape
    fan = GROUP_ROWS // cap
    groups = devices // fan
    group_bits = groups.bit_length() - 1
    my_group = me // fan
    half = me % 2
    partner = me + 1 - 2 * half
    my_place = me // 2
    twin = {"parts": 1 - lax.axis_index("parts")}
    sizes = sorted(set(caps))
    adaptive = places is not None

    def size_at(place):
        out = 0
        for rank, size in enumerate(caps):
            out = out + jnp.where(place == places[rank], size, 0)
        return out

    def with_size(place, act):
        if not adaptive:
            act(cap)
            return
        size = size_at(place)
        for case in sizes:
            pl.when(size == case)(functools.partial(act, case))

    def peer(mask):
        return flipped(me, mask, bits)

    def group_of(mask):
        return flipped(my_group, mask, group_bits)

    if adaptive:
        least = sizes[0]

        @pl.when(size_at(my_place) < cap)
        def clear():
            for ref in (own, other):
                ref[:, least:, :] = jnp.zeros((devices, cap - least, width), jnp.bfloat16)

    barrier = pltpu.get_barrier_semaphore()
    if adaptive:
        pl.semaphore_signal(barrier, inc=1, device_id=twin, device_id_type=MESH)
    for mask in range(1, devices):
        pl.semaphore_signal(barrier, inc=1, device_id={"wide": peer(mask)}, device_id_type=MESH)

    cluster = cluster_ref[...]
    onehot = lax.broadcasted_iota(jnp.int32, (clusters, rows), 0) == cluster
    ones = jnp.where(onehot, 1.0, 0.0)
    before = (
        lax.broadcasted_iota(jnp.int32, (rows, rows), 0)
        < lax.broadcasted_iota(jnp.int32, (rows, rows), 1)
    )
    prefix = jnp.dot(
        ones.astype(jnp.bfloat16),
        jnp.where(before, 1.0, 0.0).astype(jnp.bfloat16),
        preferred_element_type=jnp.float32,
    )
    within = jnp.sum(prefix * ones, axis=0, keepdims=True).astype(jnp.int32)
    place = within >> 1
    count_out[...] = jnp.broadcast_to(jnp.sum(ones, axis=1, keepdims=True), (clusters, LANES))
    count_in[me] = count_out[...]
    pl.semaphore_wait(barrier, devices if adaptive else devices - 1)

    def count_copy(mask):
        return pltpu.make_async_remote_copy(
            src_ref=count_out, dst_ref=count_in.at[me],
            send_sem=count_send.at[mask], recv_sem=count_recv.at[mask],
            device_id={"wide": peer(mask)}, device_id_type=MESH,
        )

    for mask in reversed(range(1, devices)):
        count_copy(mask).start()

    values = emb_ref[...].astype(jnp.float32)
    scale = lax.rsqrt(jnp.sum(values * values, axis=1, keepdims=True) + EPSILON)
    unit[...] = (values * scale).astype(jnp.bfloat16)

    for mask in range(1, devices):
        count_copy(mask).wait_recv()
    cluster_id = lax.broadcasted_iota(jnp.int32, (clusters, LANES), 0)
    flag_copy = pltpu.make_async_remote_copy(
        src_ref=flag_out, dst_ref=flag_in, send_sem=flag_send, recv_sem=flag_recv,
        device_id=twin, device_id_type=MESH,
    )
    if adaptive:
        most = jnp.max(count_in[...], axis=0)
        rank = jnp.zeros((clusters, LANES), jnp.int32)
        for c in range(clusters):
            against = most[c : c + 1]
            ahead = (against > most) | ((against == most) & (cluster_id > c))
            rank = rank + jnp.where(ahead, 1, 0)
        home = jnp.zeros((clusters, LANES), jnp.int32)
        room = jnp.zeros((clusters, LANES), jnp.float32)
        for r in range(clusters):
            home = home + jnp.where(rank == r, places[r], 0)
            room = room + jnp.where(rank == r, 2.0 * caps[r], 0.0)
        excess = jnp.max(jnp.where(most > room, 1.0, 0.0), axis=0, keepdims=True)
        flag_out[...] = jnp.broadcast_to(excess, (8, LANES))
        flag_copy.start()
        wide_home = jnp.concatenate([home] * (rows // LANES), axis=1)
        label = jnp.sum(jnp.where(onehot, wide_home, 0), axis=0, keepdims=True)
    else:
        home = cluster_id
        label = cluster
    target = 2 * label + (within & 1)
    position = target * cap + place
    at_home = home == my_place
    home_count[...] = jnp.broadcast_to(
        jnp.sum(jnp.where(at_home, count_in[...], 0.0), axis=1, keepdims=True),
        (devices, 8, LANES),
    )
    sharp = LOG2E * jnp.sum(jnp.where(at_home, sharp_ref[...], 0.0), axis=0, keepdims=True)

    def row_copy(mask, size):
        to = peer(mask)
        return pltpu.make_async_remote_copy(
            src_ref=send.at[to, pl.ds(0, size)], dst_ref=own.at[me, pl.ds(0, size)],
            send_sem=row_send.at[mask], recv_sem=row_recv.at[mask],
            device_id={"wide": to}, device_id_type=MESH,
        )

    def pass_copy(mask, landing, size):
        origin = peer(mask)
        return pltpu.make_async_remote_copy(
            src_ref=own.at[origin, pl.ds(0, size)], dst_ref=other.at[origin, pl.ds(0, size)],
            send_sem=pass_send.at[mask], recv_sem=pass_recv.at[landing],
            device_id={"wide": partner}, device_id_type=MESH,
        )

    def back_copy(mask):
        to = peer(mask)
        return pltpu.make_async_remote_copy(
            src_ref=back_out.at[(to * cap) // LANES], dst_ref=back_in.at[me],
            send_sem=back_send.at[mask], recv_sem=back_recv.at[mask],
            device_id={"wide": to}, device_id_type=MESH,
        )

    for step in reversed(range(groups)):
        goal = group_of(step)
        slot = lax.broadcasted_iota(jnp.int32, (GROUP_ROWS, rows), 0) + goal * GROUP_ROWS
        pick = jnp.where(slot == position, 1.0, 0.0).astype(jnp.bfloat16)
        packed = jnp.dot(pick, unit[...], preferred_element_type=jnp.float32)
        send[pl.ds(goal * fan, fan)] = packed.astype(jnp.bfloat16).reshape(fan, cap, width)
        for g in range(fan):
            mask = step * fan + g
            if mask:
                with_size(peer(mask) // 2, lambda size: row_copy(mask, size).start())
            else:
                own[me] = send[me]

    wide_sharp = jnp.concatenate([sharp] * (GROUP_ROWS // LANES), axis=1)
    total[...] = jnp.zeros_like(total)
    inner = lax.broadcasted_iota(jnp.int32, (cap, LANES), 0).astype(jnp.float32)
    skip = (
        lax.broadcasted_iota(jnp.int32, (GROUP_ROWS, GROUP_ROWS), 0)
        == lax.broadcasted_iota(jnp.int32, (GROUP_ROWS, GROUP_ROWS), 1)
    )
    half_f = half.astype(jnp.float32)

    def add_block(rows_ref, bias_ref, j, i, diagonal=False):
        left = rows_ref[pl.ds(j * fan, fan)].reshape(GROUP_ROWS, width)
        right = own[pl.ds(i * fan, fan)].reshape(GROUP_ROWS, width)
        similarity = lax.dot_general(
            left, right, (((1,), (1,)), ((), ())), preferred_element_type=jnp.float32
        )
        bias = bias_ref[pl.ds(j * fan, fan)].reshape(GROUP_ROWS, LANES)
        bias = jnp.concatenate([bias] * (GROUP_ROWS // LANES), axis=1)
        kernel = jnp.exp2(similarity * wide_sharp + bias)
        if diagonal:
            kernel = jnp.where(skip, 0.0, kernel)
        total[i] += jnp.sum(kernel.reshape(GROUP_ROWS // 8, 8, GROUP_ROWS), axis=0)

    for step in range(groups):

        def land(size):
            for g in range(fan):
                mask = step * fan + g
                if mask:
                    row_copy(mask, size).wait_recv()
                pass_copy(mask, mask ^ 1, size).start()

        with_size(my_place, land)
        for g in range(fan):
            mask = step * fan + g
            origin = peer(mask)
            count = home_count[origin][0:1]
            own_live = jnp.floor((count + 1.0 - half_f) * 0.5)
            own_bias[origin] = jnp.where(inner < own_live, -sharp, DEAD)
            other_bias[origin] = jnp.where(inner < count - own_live, -sharp, DEAD)
        here = group_of(step)
        add_block(own, own_bias, here, here, diagonal=True)

        def passed(size):
            for g in range(fan):
                pass_copy(step * fan + g, step * fan + g, size).wait_recv()

        with_size(my_place, passed)
        add_block(other, other_bias, here, here)
        if step:

            def earlier(index, carry):
                there = group_of(index)
                add_block(own, own_bias, here, there)
                add_block(other, other_bias, here, there)
                add_block(own, own_bias, there, here)
                add_block(other, other_bias, there, here)
                return carry

            lax.fori_loop(0, step, earlier, 0)

    members = jnp.sum(home_count[...], axis=0)[0:1]
    divisor = jnp.maximum(members - 1.0, 1.0)
    pieces = GROUP_ROWS // LANES
    for i in range(groups):
        sums = jnp.sum(total[i], axis=0, keepdims=True)
        for piece in range(pieces):
            density = jnp.log(sums[:, piece * LANES : (piece + 1) * LANES] / divisor)
            back_out[i * pieces + piece] = jnp.broadcast_to(density, (8, LANES))
    for mask in range(1, devices):
        back_copy(mask).start()
    back_in[me] = back_out[(me * cap) // LANES]

    lane = place + (me * cap) % LANES
    choose = jnp.where(lax.broadcasted_iota(jnp.int32, (LANES, rows), 0) == lane, 1.0, 0.0)
    mine = lax.broadcasted_iota(jnp.int32, (devices, rows), 0) == target
    for mask in range(1, devices):
        back_copy(mask).wait_recv()
    gathered = jnp.dot(
        back_in[...][:, 0, :], choose,
        preferred_element_type=jnp.float32, precision=lax.Precision.HIGHEST,
    )
    out_ref[...] = jnp.sum(jnp.where(mine, gathered, 0.0), axis=0, keepdims=True)

    def passed_on(size):
        for mask in range(devices):
            pass_copy(mask, mask ^ 1, size).wait_send()

    with_size(my_place, passed_on)
    for mask in range(1, devices):
        count_copy(mask).wait_send()
        with_size(peer(mask) // 2, lambda size: row_copy(mask, size).wait_send())
        back_copy(mask).wait_send()
    if adaptive:
        flag_copy.wait()
        flag_ref[...] = jnp.maximum(flag_out[...], flag_in[...])
    else:
        flag_ref[...] = jnp.zeros((8, LANES), jnp.float32)


def swapped(block, axis, bit):
    count = lax.axis_size(axis)
    route = []
    for low in range(count):
        high = low | 1 << bit
        if high != low and high < count:
            route += [(low, high), (high, low)]
    return lax.ppermute(block, axis, route)


def unit_rows(embeddings):
    values = embeddings.astype(jnp.float32)
    scaled = values * lax.rsqrt(jnp.sum(values * values, axis=1, keepdims=True) + EPSILON)
    return scaled.astype(jnp.bfloat16)


def kernel_sums(left, left_live, right, right_live, sharp_value, block_size, skip_self):
    width = left.shape[1]
    left_count = left.shape[0] // block_size
    right_count = right.shape[0] // block_size
    left_blocks = left.reshape(left_count, block_size, width)
    left_masks = left_live.reshape(left_count, block_size)
    right_blocks = right.reshape(right_count, block_size, width)
    right_masks = right_live.reshape(right_count, block_size)
    offsets = jnp.arange(block_size, dtype=jnp.int32)

    def outer_step(column_total, left_item):
        left_index, left_block, left_mask = left_item

        def inner_step(row_total, right_item):
            right_index, right_block, right_mask = right_item
            similarity = jnp.einsum(
                "ie,je->ij", left_block, right_block, preferred_element_type=jnp.float32
            )
            kernel = (
                jnp.exp(sharp_value * (similarity - 1.0)) * left_mask[:, None] * right_mask[None, :]
            )
            if skip_self:
                diagonal = (left_index * block_size + offsets)[:, None] == (
                    right_index * block_size + offsets
                )[None, :]
                kernel = jnp.where(diagonal, 0.0, kernel)
            return (row_total + jnp.sum(kernel, axis=1), jnp.sum(kernel, axis=0))

        row_total, column_part = lax.scan(
            inner_step,
            jnp.zeros((block_size,), jnp.float32),
            (jnp.arange(right_count, dtype=jnp.int32), right_blocks, right_masks),
        )
        return (column_total + column_part, row_total)

    column_total, row_totals = lax.scan(
        outer_step,
        jnp.zeros((right_count, block_size), jnp.float32),
        (jnp.arange(left_count, dtype=jnp.int32), left_blocks, left_masks),
    )
    return (row_totals.reshape(left.shape[0]), column_total.reshape(right.shape[0]))


def any_counts(embeddings, cluster_of, sharpness):
    devices = lax.axis_size("wide")
    device_index = lax.axis_index("wide")
    local_rows = embeddings.shape[0]
    width = embeddings.shape[1]
    clusters = sharpness.shape[0]
    capacity = local_rows // clusters
    slots = devices * capacity
    block_size = min(512, slots // 2)
    unit_vectors = unit_rows(embeddings)
    onehot_int = (cluster_of[:, None] == jnp.arange(clusters, dtype=jnp.int32)[None, :]).astype(
        jnp.int32
    )
    within = jnp.sum((jnp.cumsum(onehot_int, axis=0) - onehot_int) * onehot_int, axis=1)
    target = 2 * cluster_of + within % 2
    position = target * capacity + within // 2
    send_rows = jnp.zeros((slots, width), jnp.bfloat16).at[position].set(unit_vectors)
    per_cluster = jnp.sum(onehot_int, axis=0)
    per_target = jnp.stack([(per_cluster + 1) // 2, per_cluster // 2], axis=1).reshape(devices)
    slot_column = jnp.arange(capacity, dtype=jnp.int32)
    own_rows, own_counts = (
        lax.all_to_all(send_rows, "wide", split_axis=0, concat_axis=0, tiled=True),
        lax.all_to_all(
            per_target.astype(jnp.bfloat16), "wide", split_axis=0, concat_axis=0, tiled=True
        ),
    )
    own_live = (
        (slot_column[None, :] < own_counts.astype(jnp.int32)[:, None])
        .astype(jnp.float32)
        .reshape(slots)
    )
    partner_rows, partner_flags = swapped((own_rows, own_live.astype(jnp.bfloat16)), "wide", 0)
    partner_live = partner_flags.astype(jnp.float32)
    sharp_value = lax.dynamic_slice_in_dim(sharpness, device_index // 2, 1, 0)[0]
    members = jnp.sum(own_live) + jnp.sum(partner_live)
    divisor = jnp.maximum(members - 1.0, 1.0)
    self_rows, unused_columns = kernel_sums(
        own_rows, own_live, own_rows, own_live, sharp_value, block_size, True
    )
    cross_rows, other_columns = kernel_sums(
        own_rows, own_live, partner_rows, partner_live, sharp_value, block_size, False
    )
    kernel_total = self_rows + cross_rows
    density_here = jnp.log((kernel_total + (1.0 - own_live)) / divisor)
    returned = lax.all_to_all(density_here, "wide", split_axis=0, concat_axis=0, tiled=True)
    return jnp.take(returned, position, axis=0)


def per_device(embeddings, cluster_of, sharpness):
    devices = lax.axis_size("wide")
    rows, width = embeddings.shape
    clusters = sharpness.shape[0]
    cap = max(16, rows // clusters)
    slots = devices * cap
    vmem = pl.BlockSpec(memory_space=pltpu.VMEM)
    dma = pltpu.SemaphoreType.DMA((devices,))
    adaptive = clusters == len(RANK_CAPS) and cap == max(RANK_CAPS)
    caps = RANK_CAPS if adaptive else (cap,) * clusters
    places = RANK_PLACES if adaptive else None
    out, flag = pl.pallas_call(
        functools.partial(body, devices, clusters, cap, caps, places),
        out_shape=(
            jax.ShapeDtypeStruct((1, rows), jnp.float32),
            jax.ShapeDtypeStruct((8, LANES), jnp.float32),
        ),
        in_specs=[vmem, vmem, vmem],
        out_specs=(vmem, vmem),
        scratch_shapes=[
            pltpu.VMEM((rows, width), jnp.bfloat16),
            pltpu.VMEM((devices, cap, width), jnp.bfloat16),
            pltpu.VMEM((devices, cap, width), jnp.bfloat16),
            pltpu.VMEM((devices, cap, width), jnp.bfloat16),
            pltpu.VMEM((clusters, LANES), jnp.float32),
            pltpu.VMEM((devices, clusters, LANES), jnp.float32),
            pltpu.VMEM((devices, 8, LANES), jnp.float32),
            pltpu.VMEM((devices, cap, LANES), jnp.float32),
            pltpu.VMEM((devices, cap, LANES), jnp.float32),
            pltpu.VMEM((slots // GROUP_ROWS, 8, GROUP_ROWS), jnp.float32),
            pltpu.VMEM((slots // LANES, 8, LANES), jnp.float32),
            pltpu.VMEM((devices, 8, LANES), jnp.float32),
            pltpu.VMEM((8, LANES), jnp.float32),
            pltpu.VMEM((8, LANES), jnp.float32),
            dma, dma, dma, dma, dma, dma, dma, dma,
            pltpu.SemaphoreType.DMA, pltpu.SemaphoreType.DMA,
        ],
        compiler_params=pltpu.CompilerParams(
            collective_id=0, has_side_effects=True, vmem_limit_bytes=40 * 1024 * 1024
        ),
    )(embeddings, cluster_of.reshape(1, rows), sharpness.reshape(clusters, 1))
    out = out.reshape(rows)
    if not adaptive:
        return out
    return lax.cond(
        flag[0, 0] > 0.0,
        lambda values, ids, sharp, ready: any_counts(values, ids, sharp),
        lambda values, ids, sharp, ready: ready,
        embeddings, cluster_of, sharpness, out,
    )


def solution(mesh):
    in_specs = (P(("parts", "wide"), None), P(("parts", "wide")), P("parts"))
    out_specs = P(("parts", "wide"))
    return jax.shard_map(
        per_device, mesh=mesh, in_specs=in_specs, out_specs=out_specs, check_vma=False
    )
```

```python
import functools

import jax
import jax.numpy as jnp
from jax import lax
from jax.experimental import pallas as pl
from jax.experimental.pallas import tpu as pltpu
from jax.sharding import PartitionSpec as P

EPSILON = 1e-06
LOG2E = 1.4426950408889634
DEAD = -1e30
LANES = 128
GROUP_ROWS = 256
MESH = pl.DeviceIdType.MESH
RANK_CAPS = (64, 64, 64, 64, 48, 48, 32, 32)
RANK_PLACES = (0, 4, 5, 1, 2, 6, 3, 7)


def flipped(value, mask, bits):
    out = 0
    for k in range(bits):
        left = (value // (1 << k)) % 2
        right = (mask // (1 << k)) % 2
        out = out + (left + right - 2 * left * right) * (1 << k)
    return out


def body(
    devices, clusters, cap, caps, places,
    emb_ref, cluster_ref, sharp_ref, out_ref, flag_ref,
    unit, send, own, other, count_out, count_in, home_count, own_bias, other_bias, total,
    back_out, back_in, flag_out, flag_in,
    row_send, row_recv, count_send, count_recv, pass_send, pass_recv, back_send, back_recv,
    flag_send, flag_recv,
):
    bits = devices.bit_length() - 1
    me = lax.axis_index("wide")
    rows, width = emb_ref.shape
    fan = GROUP_ROWS // cap
    groups = devices // fan
    group_bits = groups.bit_length() - 1
    my_group = me // fan
    half = me % 2
    partner = me + 1 - 2 * half
    my_place = me // 2
    twin = {"parts": 1 - lax.axis_index("parts")}
    sizes = sorted(set(caps))
    adaptive = places is not None

    def size_at(place):
        out = 0
        for rank, size in enumerate(caps):
            out = out + jnp.where(place == places[rank], size, 0)
        return out

    def with_size(place, act):
        if not adaptive:
            act(cap)
            return
        size = size_at(place)
        for case in sizes:
            pl.when(size == case)(functools.partial(act, case))

    def peer(mask):
        return flipped(me, mask, bits)

    def group_of(mask):
        return flipped(my_group, mask, group_bits)

    if adaptive:
        least = sizes[0]

        @pl.when(size_at(my_place) < cap)
        def clear():
            for ref in (own, other):
                ref[:, least:, :] = jnp.zeros((devices, cap - least, width), jnp.bfloat16)

    barrier = pltpu.get_barrier_semaphore()
    if adaptive:
        pl.semaphore_signal(barrier, inc=1, device_id=twin, device_id_type=MESH)
    for mask in range(1, devices):
        pl.semaphore_signal(barrier, inc=1, device_id={"wide": peer(mask)}, device_id_type=MESH)

    cluster = cluster_ref[...]
    onehot = lax.broadcasted_iota(jnp.int32, (clusters, rows), 0) == cluster
    ones = jnp.where(onehot, 1.0, 0.0)
    before = (
        lax.broadcasted_iota(jnp.int32, (rows, rows), 0)
        < lax.broadcasted_iota(jnp.int32, (rows, rows), 1)
    )
    prefix = jnp.dot(
        ones.astype(jnp.bfloat16),
        jnp.where(before, 1.0, 0.0).astype(jnp.bfloat16),
        preferred_element_type=jnp.float32,
    )
    within = jnp.sum(prefix * ones, axis=0, keepdims=True).astype(jnp.int32)
    place = within >> 1
    count_out[...] = jnp.broadcast_to(jnp.sum(ones, axis=1, keepdims=True), (clusters, LANES))
    count_in[me] = count_out[...]
    pl.semaphore_wait(barrier, devices if adaptive else devices - 1)

    def count_copy(mask):
        return pltpu.make_async_remote_copy(
            src_ref=count_out, dst_ref=count_in.at[me],
            send_sem=count_send.at[mask], recv_sem=count_recv.at[mask],
            device_id={"wide": peer(mask)}, device_id_type=MESH,
        )

    for mask in reversed(range(1, devices)):
        count_copy(mask).start()

    values = emb_ref[...].astype(jnp.float32)
    scale = lax.rsqrt(jnp.sum(values * values, axis=1, keepdims=True) + EPSILON)
    unit[...] = (values * scale).astype(jnp.bfloat16)

    for mask in range(1, devices):
        count_copy(mask).wait_recv()
    cluster_id = lax.broadcasted_iota(jnp.int32, (clusters, LANES), 0)
    flag_copy = pltpu.make_async_remote_copy(
        src_ref=flag_out, dst_ref=flag_in, send_sem=flag_send, recv_sem=flag_recv,
        device_id=twin, device_id_type=MESH,
    )
    if adaptive:
        most = jnp.max(count_in[...], axis=0)
        rank = jnp.zeros((clusters, LANES), jnp.int32)
        for c in range(clusters):
            against = most[c : c + 1]
            ahead = (against > most) | ((against == most) & (cluster_id > c))
            rank = rank + jnp.where(ahead, 1, 0)
        home = jnp.zeros((clusters, LANES), jnp.int32)
        room = jnp.zeros((clusters, LANES), jnp.float32)
        for r in range(clusters):
            home = home + jnp.where(rank == r, places[r], 0)
            room = room + jnp.where(rank == r, 2.0 * caps[r], 0.0)
        excess = jnp.max(jnp.where(most > room, 1.0, 0.0), axis=0, keepdims=True)
        flag_out[...] = jnp.broadcast_to(excess, (8, LANES))
        flag_copy.start()
        wide_home = jnp.concatenate([home] * (rows // LANES), axis=1)
        label = jnp.sum(jnp.where(onehot, wide_home, 0), axis=0, keepdims=True)
    else:
        home = cluster_id
        label = cluster
    target = 2 * label + (within & 1)
    position = target * cap + place
    at_home = home == my_place
    home_count[...] = jnp.broadcast_to(
        jnp.sum(jnp.where(at_home, count_in[...], 0.0), axis=1, keepdims=True),
        (devices, 8, LANES),
    )
    sharp = LOG2E * jnp.sum(jnp.where(at_home, sharp_ref[...], 0.0), axis=0, keepdims=True)

    def row_copy(mask, size):
        to = peer(mask)
        return pltpu.make_async_remote_copy(
            src_ref=send.at[to, pl.ds(0, size)], dst_ref=own.at[me, pl.ds(0, size)],
            send_sem=row_send.at[mask], recv_sem=row_recv.at[mask],
            device_id={"wide": to}, device_id_type=MESH,
        )

    def pass_copy(mask, landing, size):
        origin = peer(mask)
        return pltpu.make_async_remote_copy(
            src_ref=own.at[origin, pl.ds(0, size)], dst_ref=other.at[origin, pl.ds(0, size)],
            send_sem=pass_send.at[mask], recv_sem=pass_recv.at[landing],
            device_id={"wide": partner}, device_id_type=MESH,
        )

    def back_copy(mask):
        to = peer(mask)
        return pltpu.make_async_remote_copy(
            src_ref=back_out.at[(to * cap) // LANES], dst_ref=back_in.at[me],
            send_sem=back_send.at[mask], recv_sem=back_recv.at[mask],
            device_id={"wide": to}, device_id_type=MESH,
        )

    for step in ((2, 3, 1, 0) if groups == 4 else reversed(range(groups))):
        goal = group_of(step)
        slot = lax.broadcasted_iota(jnp.int32, (GROUP_ROWS, rows), 0) + goal * GROUP_ROWS
        pick = jnp.where(slot == position, 1.0, 0.0).astype(jnp.bfloat16)
        packed = jnp.dot(pick, unit[...], preferred_element_type=jnp.float32)
        send[pl.ds(goal * fan, fan)] = packed.astype(jnp.bfloat16).reshape(fan, cap, width)
        for g in range(fan):
            mask = step * fan + g
            if mask:
                with_size(peer(mask) // 2, lambda size: row_copy(mask, size).start())
            else:
                own[me] = send[me]

    wide_sharp = jnp.concatenate([sharp] * (GROUP_ROWS // LANES), axis=1)
    total[...] = jnp.zeros_like(total)
    inner = lax.broadcasted_iota(jnp.int32, (cap, LANES), 0).astype(jnp.float32)
    skip = (
        lax.broadcasted_iota(jnp.int32, (GROUP_ROWS, GROUP_ROWS), 0)
        == lax.broadcasted_iota(jnp.int32, (GROUP_ROWS, GROUP_ROWS), 1)
    )
    half_f = half.astype(jnp.float32)

    def add_block(rows_ref, bias_ref, j, i, diagonal=False):
        left = rows_ref[pl.ds(j * fan, fan)].reshape(GROUP_ROWS, width)
        right = own[pl.ds(i * fan, fan)].reshape(GROUP_ROWS, width)
        similarity = lax.dot_general(
            left, right, (((1,), (1,)), ((), ())), preferred_element_type=jnp.float32
        )
        bias = bias_ref[pl.ds(j * fan, fan)].reshape(GROUP_ROWS, LANES)
        bias = jnp.concatenate([bias] * (GROUP_ROWS // LANES), axis=1)
        kernel = jnp.exp2(similarity * wide_sharp + bias)
        if diagonal:
            kernel = jnp.where(skip, 0.0, kernel)
        total[i] += jnp.sum(kernel.reshape(GROUP_ROWS // 8, 8, GROUP_ROWS), axis=0)

    for step in range(groups):

        def land(size):
            for g in range(fan):
                mask = step * fan + g
                if mask:
                    row_copy(mask, size).wait_recv()
                pass_copy(mask, mask ^ 1, size).start()

        with_size(my_place, land)
        for g in range(fan):
            mask = step * fan + g
            origin = peer(mask)
            count = home_count[origin][0:1]
            own_live = jnp.floor((count + 1.0 - half_f) * 0.5)
            own_bias[origin] = jnp.where(inner < own_live, -sharp, DEAD)
            other_bias[origin] = jnp.where(inner < count - own_live, -sharp, DEAD)
        here = group_of(step)
        add_block(own, own_bias, here, here, diagonal=True)

        def passed(size):
            for g in range(fan):
                pass_copy(step * fan + g, step * fan + g, size).wait_recv()

        with_size(my_place, passed)
        add_block(other, other_bias, here, here)
        if step:

            def earlier(index, carry):
                there = group_of(index)
                add_block(own, own_bias, here, there)
                add_block(other, other_bias, here, there)
                add_block(own, own_bias, there, here)
                add_block(other, other_bias, there, here)
                return carry

            lax.fori_loop(0, step, earlier, 0)

    members = jnp.sum(home_count[...], axis=0)[0:1]
    divisor = jnp.maximum(members - 1.0, 1.0)
    pieces = GROUP_ROWS // LANES
    for i in range(groups):
        sums = jnp.sum(total[i], axis=0, keepdims=True)
        for piece in range(pieces):
            density = jnp.log(sums[:, piece * LANES : (piece + 1) * LANES] / divisor)
            back_out[i * pieces + piece] = jnp.broadcast_to(density, (8, LANES))
    for mask in range(1, devices):
        back_copy(mask).start()
    back_in[me] = back_out[(me * cap) // LANES]

    lane = place + (me * cap) % LANES
    choose = jnp.where(lax.broadcasted_iota(jnp.int32, (LANES, rows), 0) == lane, 1.0, 0.0)
    mine = lax.broadcasted_iota(jnp.int32, (devices, rows), 0) == target
    for mask in range(1, devices):
        back_copy(mask).wait_recv()
    gathered = jnp.dot(
        back_in[...][:, 0, :], choose,
        preferred_element_type=jnp.float32, precision=lax.Precision.HIGHEST,
    )
    out_ref[...] = jnp.sum(jnp.where(mine, gathered, 0.0), axis=0, keepdims=True)

    def passed_on(size):
        for mask in range(devices):
            pass_copy(mask, mask ^ 1, size).wait_send()

    with_size(my_place, passed_on)
    for mask in range(1, devices):
        count_copy(mask).wait_send()
        with_size(peer(mask) // 2, lambda size: row_copy(mask, size).wait_send())
        back_copy(mask).wait_send()
    if adaptive:
        flag_copy.wait()
        flag_ref[...] = jnp.maximum(flag_out[...], flag_in[...])
    else:
        flag_ref[...] = jnp.zeros((8, LANES), jnp.float32)


def swapped(block, axis, bit):
    count = lax.axis_size(axis)
    route = []
    for low in range(count):
        high = low | 1 << bit
        if high != low and high < count:
            route += [(low, high), (high, low)]
    return lax.ppermute(block, axis, route)


def unit_rows(embeddings):
    values = embeddings.astype(jnp.float32)
    scaled = values * lax.rsqrt(jnp.sum(values * values, axis=1, keepdims=True) + EPSILON)
    return scaled.astype(jnp.bfloat16)


def kernel_sums(left, left_live, right, right_live, sharp_value, block_size, skip_self):
    width = left.shape[1]
    left_count = left.shape[0] // block_size
    right_count = right.shape[0] // block_size
    left_blocks = left.reshape(left_count, block_size, width)
    left_masks = left_live.reshape(left_count, block_size)
    right_blocks = right.reshape(right_count, block_size, width)
    right_masks = right_live.reshape(right_count, block_size)
    offsets = jnp.arange(block_size, dtype=jnp.int32)

    def outer_step(column_total, left_item):
        left_index, left_block, left_mask = left_item

        def inner_step(row_total, right_item):
            right_index, right_block, right_mask = right_item
            similarity = jnp.einsum(
                "ie,je->ij", left_block, right_block, preferred_element_type=jnp.float32
            )
            kernel = (
                jnp.exp(sharp_value * (similarity - 1.0)) * left_mask[:, None] * right_mask[None, :]
            )
            if skip_self:
                diagonal = (left_index * block_size + offsets)[:, None] == (
                    right_index * block_size + offsets
                )[None, :]
                kernel = jnp.where(diagonal, 0.0, kernel)
            return (row_total + jnp.sum(kernel, axis=1), jnp.sum(kernel, axis=0))

        row_total, column_part = lax.scan(
            inner_step,
            jnp.zeros((block_size,), jnp.float32),
            (jnp.arange(right_count, dtype=jnp.int32), right_blocks, right_masks),
        )
        return (column_total + column_part, row_total)

    column_total, row_totals = lax.scan(
        outer_step,
        jnp.zeros((right_count, block_size), jnp.float32),
        (jnp.arange(left_count, dtype=jnp.int32), left_blocks, left_masks),
    )
    return (row_totals.reshape(left.shape[0]), column_total.reshape(right.shape[0]))


def any_counts(embeddings, cluster_of, sharpness):
    devices = lax.axis_size("wide")
    device_index = lax.axis_index("wide")
    local_rows = embeddings.shape[0]
    width = embeddings.shape[1]
    clusters = sharpness.shape[0]
    capacity = local_rows // clusters
    slots = devices * capacity
    block_size = min(512, slots // 2)
    unit_vectors = unit_rows(embeddings)
    onehot_int = (cluster_of[:, None] == jnp.arange(clusters, dtype=jnp.int32)[None, :]).astype(
        jnp.int32
    )
    within = jnp.sum((jnp.cumsum(onehot_int, axis=0) - onehot_int) * onehot_int, axis=1)
    target = 2 * cluster_of + within % 2
    position = target * capacity + within // 2
    send_rows = jnp.zeros((slots, width), jnp.bfloat16).at[position].set(unit_vectors)
    per_cluster = jnp.sum(onehot_int, axis=0)
    per_target = jnp.stack([(per_cluster + 1) // 2, per_cluster // 2], axis=1).reshape(devices)
    slot_column = jnp.arange(capacity, dtype=jnp.int32)
    own_rows, own_counts = (
        lax.all_to_all(send_rows, "wide", split_axis=0, concat_axis=0, tiled=True),
        lax.all_to_all(
            per_target.astype(jnp.bfloat16), "wide", split_axis=0, concat_axis=0, tiled=True
        ),
    )
    own_live = (
        (slot_column[None, :] < own_counts.astype(jnp.int32)[:, None])
        .astype(jnp.float32)
        .reshape(slots)
    )
    partner_rows, partner_flags = swapped((own_rows, own_live.astype(jnp.bfloat16)), "wide", 0)
    partner_live = partner_flags.astype(jnp.float32)
    sharp_value = lax.dynamic_slice_in_dim(sharpness, device_index // 2, 1, 0)[0]
    members = jnp.sum(own_live) + jnp.sum(partner_live)
    divisor = jnp.maximum(members - 1.0, 1.0)
    self_rows, unused_columns = kernel_sums(
        own_rows, own_live, own_rows, own_live, sharp_value, block_size, True
    )
    cross_rows, other_columns = kernel_sums(
        own_rows, own_live, partner_rows, partner_live, sharp_value, block_size, False
    )
    kernel_total = self_rows + cross_rows
    density_here = jnp.log((kernel_total + (1.0 - own_live)) / divisor)
    returned = lax.all_to_all(density_here, "wide", split_axis=0, concat_axis=0, tiled=True)
    return jnp.take(returned, position, axis=0)


def per_device(embeddings, cluster_of, sharpness):
    devices = lax.axis_size("wide")
    rows, width = embeddings.shape
    clusters = sharpness.shape[0]
    cap = max(16, rows // clusters)
    slots = devices * cap
    vmem = pl.BlockSpec(memory_space=pltpu.VMEM)
    dma = pltpu.SemaphoreType.DMA((devices,))
    adaptive = clusters == len(RANK_CAPS) and cap == max(RANK_CAPS)
    caps = RANK_CAPS if adaptive else (cap,) * clusters
    places = RANK_PLACES if adaptive else None
    out, flag = pl.pallas_call(
        functools.partial(body, devices, clusters, cap, caps, places),
        out_shape=(
            jax.ShapeDtypeStruct((1, rows), jnp.float32),
            jax.ShapeDtypeStruct((8, LANES), jnp.float32),
        ),
        in_specs=[vmem, vmem, vmem],
        out_specs=(vmem, vmem),
        scratch_shapes=[
            pltpu.VMEM((rows, width), jnp.bfloat16),
            pltpu.VMEM((devices, cap, width), jnp.bfloat16),
            pltpu.VMEM((devices, cap, width), jnp.bfloat16),
            pltpu.VMEM((devices, cap, width), jnp.bfloat16),
            pltpu.VMEM((clusters, LANES), jnp.float32),
            pltpu.VMEM((devices, clusters, LANES), jnp.float32),
            pltpu.VMEM((devices, 8, LANES), jnp.float32),
            pltpu.VMEM((devices, cap, LANES), jnp.float32),
            pltpu.VMEM((devices, cap, LANES), jnp.float32),
            pltpu.VMEM((slots // GROUP_ROWS, 8, GROUP_ROWS), jnp.float32),
            pltpu.VMEM((slots // LANES, 8, LANES), jnp.float32),
            pltpu.VMEM((devices, 8, LANES), jnp.float32),
            pltpu.VMEM((8, LANES), jnp.float32),
            pltpu.VMEM((8, LANES), jnp.float32),
            dma, dma, dma, dma, dma, dma, dma, dma,
            pltpu.SemaphoreType.DMA, pltpu.SemaphoreType.DMA,
        ],
        compiler_params=pltpu.CompilerParams(
            collective_id=0, has_side_effects=True, vmem_limit_bytes=40 * 1024 * 1024
        ),
    )(embeddings, cluster_of.reshape(1, rows), sharpness.reshape(clusters, 1))
    out = out.reshape(rows)
    if not adaptive:
        return out
    return lax.cond(
        flag[0, 0] > 0.0,
        lambda values, ids, sharp, ready: any_counts(values, ids, sharp),
        lambda values, ids, sharp, ready: ready,
        embeddings, cluster_of, sharpness, out,
    )


def solution(mesh):
    in_specs = (P(("parts", "wide"), None), P(("parts", "wide")), P("parts"))
    out_specs = P(("parts", "wide"))
    return jax.shard_map(
        per_device, mesh=mesh, in_specs=in_specs, out_specs=out_specs, check_vma=False
    )
```
